256 devices in a mesh: row: 16 (over y, x_hi, core), col: 16 (over x_lo, z).
Axes of the slice: x: 4 (x_hi: 2, x_lo: 2; x = x_hi * 2 + x_lo), y: 4, z: 8, core: 2. Of those that a mesh axis runs over, the one named last changes fastest.
Arguments:
- pair_state: bfloat16 [768, 768, 128], P('row', 'col'), may hold values from -6 to 6
- residue_mask: int32 [768], replicated, may hold values 0 or 1
- weight_in: bfloat16 [2, 128, 4, 128], replicated, may hold values from -0.5 to 0.5
- weight_gate: bfloat16 [2, 128, 128], replicated, may hold values from -0.5 to 0.5
- weight_out: bfloat16 [2, 128, 128], replicated, may hold values from -0.5 to 0.5
- gain_in: float32 [2, 128], replicated, may hold values from 0.25 to 1.75
- gain_out: float32 [2, 128], replicated, may hold values from 0.25 to 1.75
Outputs:
- updated: bfloat16 [768, 768, 128], P('row', 'col')
The draws below stay inside these ranges and needn't reach their ends.
Inputs may be any that keep to these rules, and one draw needn't show every extreme that they name: `residue_mask`: 1 marks a residue present in the crop, 0 a padded one.
All inputs are finite; a program needn't handle non-finite values.
Results may differ from the reference program's by a relative error of at most 0.0095.
Values may be sent and summed in bfloat16 or wider, within the bound.
A program may use at most 128 MiB of HBM per device.

```python
import jax
import jax.numpy as jnp
from jax import lax

PAIR_WIDTH = 128
HIDDEN_SIZE = 128
RESIDUES = 768


def set_ends(values, stream_key, low, largest):
    shape = values.shape
    place = [jax.random.randint(jax.random.fold_in(stream_key, axis), (), 0, shape[axis]) for axis in range(len(shape))]
    values = values.at[tuple(place)].set(low)
    longest = shape.index(max(shape))
    place[longest] = (place[longest] + 1) % shape[longest]
    return values.at[tuple(place)].set(largest)


def block_scale(rng, dims, cuts, smallest, top_value):
    factor_of = 1.0
    for axis_at, blocks in cuts:
        draws = jax.random.uniform(jax.random.fold_in(jax.random.fold_in(rng, 6), axis_at), (blocks,), jnp.float32, smallest / len(cuts), top_value / len(cuts))
        factor_of = factor_of * jnp.repeat(jnp.exp(draws), dims[axis_at] // blocks).reshape((-1,) + (1,) * (len(dims) - 1 - axis_at))
    return factor_of


def bell_draw(rng, dims, deviation, bound, shards=(), kind=jnp.bfloat16):
    level = block_scale(rng, dims, shards, -0.22, 0.18) if shards else 1.0
    array = jax.random.normal(rng, dims, jnp.float32) * deviation * level
    return jnp.minimum(jnp.maximum(array, -bound), bound).astype(kind)


def setup_inputs(seed: int = 0) -> dict:
    arg_keys = jax.random.split(jax.random.key(seed), 8)
    pair_state = bell_draw(arg_keys[0], (RESIDUES, RESIDUES, PAIR_WIDTH), 1.0, 6.0, ((0, 16), (1, 16)))
    residue_mask = set_ends((jax.random.randint(arg_keys[1], (RESIDUES,), 0, 8) < 7).astype(jnp.int32), jax.random.fold_in(arg_keys[1], 1), 0, 1)
    weight_in = bell_draw(arg_keys[2], (2, PAIR_WIDTH, 4, HIDDEN_SIZE), PAIR_WIDTH ** -0.5, 0.5)
    weight_gate = bell_draw(arg_keys[3], (2, PAIR_WIDTH, PAIR_WIDTH), PAIR_WIDTH ** -0.5, 0.5)
    weight_out = bell_draw(arg_keys[4], (2, HIDDEN_SIZE, PAIR_WIDTH), HIDDEN_SIZE ** -0.5, 0.5)
    gain_in = jnp.clip(1.0 + 0.15 * jax.random.normal(arg_keys[5], (2, PAIR_WIDTH), jnp.float32), 0.25, 1.75)
    gain_out = jnp.clip(1.0 + 0.15 * jax.random.normal(arg_keys[6], (2, HIDDEN_SIZE), jnp.float32), 0.25, 1.75)
    return {"pair_state": pair_state, "residue_mask": residue_mask, "weight_in": weight_in, "weight_gate": weight_gate, "weight_out": weight_out, "gain_in": gain_in, "gain_out": gain_out}


epsilon = 1e-05

def normalize(values, scale_gain):
    average = lax.optimization_barrier(jnp.mean(values, axis=-1, keepdims=True))
    centered = values - average
    variance = lax.optimization_barrier(jnp.mean(centered * centered, axis=-1, keepdims=True))
    return centered * lax.rsqrt(variance + epsilon) * scale_gain

def triangle_update(current, mask_float, layer_in, layer_gate, layer_out, norm_in, norm_out, incoming):
    weights_flat = layer_in.reshape(PAIR_WIDTH, 4 * HIDDEN_SIZE)

    def project_row(inputs):
        row_values, row_mask = inputs
        normed = normalize(row_values.astype(jnp.float32), norm_in).astype(jnp.bfloat16)
        projected = jnp.dot(normed, weights_flat, preferred_element_type=jnp.float32).reshape(RESIDUES, 4, HIDDEN_SIZE)
        pair_mask = (row_mask * mask_float)[:, None]
        left_side = (jax.nn.sigmoid(projected[:, 1]) * projected[:, 0] * pair_mask).astype(jnp.bfloat16)
        right_side = (jax.nn.sigmoid(projected[:, 3]) * projected[:, 2] * pair_mask).astype(jnp.bfloat16)
        return (left_side, right_side)
    left_side, right_side = lax.map(project_row, (current, mask_float))
    left_chan = jnp.transpose(left_side, (2, 0, 1))
    right_chan = jnp.transpose(right_side, (2, 0, 1))

    def contract(inputs):
        left_one, right_one = inputs
        if incoming:
            result = jnp.dot(left_one.T, right_one, preferred_element_type=jnp.float32)
        else:
            result = jnp.dot(left_one, right_one.T, preferred_element_type=jnp.float32)
        return result.astype(jnp.bfloat16)
    mixed_all = lax.map(contract, (left_chan, right_chan))
    mixed_rows = jnp.transpose(mixed_all, (1, 2, 0))

    def finish_row(inputs):
        row_values, mixed_row = inputs
        row_float = row_values.astype(jnp.float32)
        normed = normalize(row_float, norm_in).astype(jnp.bfloat16)
        gate_value = jax.nn.sigmoid(jnp.dot(normed, layer_gate, preferred_element_type=jnp.float32))
        mixed_normed = normalize(mixed_row.astype(jnp.float32), norm_out).astype(jnp.bfloat16)
        branch = jnp.dot(mixed_normed, layer_out, preferred_element_type=jnp.float32)
        return (row_float + gate_value * branch).astype(jnp.bfloat16)
    return lax.map(finish_row, (current, mixed_rows))

def reference(pair_state, residue_mask, weight_in, weight_gate, weight_out, gain_in, gain_out):
    mask_float = residue_mask.astype(jnp.float32)
    outgoing = triangle_update(pair_state, mask_float, weight_in[0], weight_gate[0], weight_out[0], gain_in[0], gain_out[0], False)
    return triangle_update(outgoing, mask_float, weight_in[1], weight_gate[1], weight_out[1], gain_in[1], gain_out[1], True)
```

```python
import jax
import jax.numpy as jnp
from jax import lax
from jax.experimental import pallas as pl
from jax.experimental.pallas import tpu as pltpu
from jax.sharding import PartitionSpec as P

MESH = pl.DeviceIdType.MESH
F32 = jnp.float32
BF16 = jnp.bfloat16
EPS = 1e-5
COLS_OUT, ROWS_OUT, PAIR_RIGHT, PAIR_LEFT, ROWS_BACK, COLS_BACK = range(6)


def sigmoid(x):
    return 0.5 * jnp.tanh(0.5 * x) + 0.5


def norm_rows(values, gain):
    mean = jnp.sum(values, axis=0, keepdims=True) * (1.0 / 128.0)
    centered = values - mean
    var = jnp.sum(centered * centered, axis=0, keepdims=True) * (1.0 / 128.0)
    return (centered * lax.rsqrt(var + EPS) * gain).astype(BF16)


def nn(a, b):
    return lax.dot_general(a, b, (((1,), (0,)), ((), ())), preferred_element_type=F32)


def nt(a, b):
    return lax.dot_general(a, b, (((1,), (1,)), ((), ())), preferred_element_type=F32)


def tn(a, b):
    return lax.dot_general(a, b, (((0,), (0,)), ((), ())), preferred_element_type=F32)


def loop(n, body, start=0):
    def step(i, carry):
        body(i)
        return carry

    lax.fori_loop(start, n, step, 0)


def wait_bytes(ref, sem):
    pltpu.make_async_copy(ref, ref, sem).wait()


def kernel(
    x_ref, mask_ref, win_ref, wgate_ref, wout_ref, gin_ref, gout_ref, out_ref,
    perm, zt, normed, gate, maskv, wproj, wg, wo, gains,
    asend, arecv, bsend, brecv, rpair, lpair, cbuf, crecv, dsend, drecv,
    stage, send_sem, recv_sem,
):
    r = lax.axis_index("row")
    c = lax.axis_index("col")
    core = r % 2
    rb = r // 2
    z = c % 8
    xl = c // 8

    def col_peer(n):
        hop = n // 2
        away = (hop + 1) // 2 * (1 - 2 * (hop % 2))
        return (xl + n % 2) % 2 * 8 + (z + away + 8) % 8

    def row_peer(n):
        return (rb // 2 + n // 2) % 4 * 2 + (rb + n) % 2

    barrier = pltpu.get_barrier_semaphore()

    def greet(row, col):
        pl.semaphore_signal(barrier, inc=1, device_id=(row, col), device_id_type=MESH)

    loop(16, lambda n: greet(r, col_peer(n)), 1)
    loop(8, lambda n: greet(row_peer(n) * 2 + core, c), 1)
    greet(rb * 2 + 1 - core, c)

    def remote(src, dst, u, phase, q, row, col):
        return pltpu.make_async_remote_copy(
            src_ref=src, dst_ref=dst,
            send_sem=send_sem.at[u, phase, q], recv_sem=recv_sem.at[u, phase, q],
            device_id=(row, col), device_id_type=MESH,
        )

    for u in range(2):
        wt = [win_ref[u, t].astype(F32).T for t in range(4)]
        for half in range(2):
            lo, hi = wt[half], wt[half + 2]
            both = jnp.concatenate([lo.reshape(16, 1, 8, 128), hi.reshape(16, 1, 8, 128)], axis=1)
            wproj[u, half] = both.reshape(256, 128).astype(BF16)
        wg[u] = wgate_ref[u].astype(F32).T.astype(BF16)
        wo[u] = wout_ref[u].astype(F32).T.astype(BF16)
        gains[u, 0] = jnp.broadcast_to(gin_ref[u : u + 1, :], (128, 128)).T
        gains[u, 1] = jnp.broadcast_to(gout_ref[u : u + 1, :], (128, 128)).T

    mask_row = jnp.broadcast_to(mask_ref[...].astype(F32), (8, 768)).astype(BF16)
    place = lax.broadcasted_iota(jnp.int32, (768, 128), 0)
    lane = lax.broadcasted_iota(jnp.int32, (768, 128), 1)
    col_masks = [
        nn(mask_row, (place == c * 48 + kh * 16 + (lane & 15)).astype(F32).astype(BF16)) for kh in range(3)
    ]

    def fill_masks(ihg):
        rows = nn(mask_row, (place == r * 48 + ihg * 8 + (lane >> 4)).astype(F32).astype(BF16))
        for kh in range(3):
            maskv[ihg // 2 * 3 + kh, ihg % 2] = rows * col_masks[kh]

    loop(6, fill_masks)

    def load_tile(ihg):
        for kh in range(3):
            block = x_ref[pl.ds(ihg * 8, 8), kh * 16 : kh * 16 + 16, :].reshape(128, 128)
            zt[ihg // 2 * 3 + kh, ihg % 2] = block.astype(F32).T

    loop(6, load_tile)

    def load_zt(i):
        return jnp.concatenate([zt[i, 0], zt[i, 1]], axis=1)

    def wide(block):
        return jnp.concatenate([block, block], axis=1)

    def project(u, q, kh, values):
        i = q * 3 + kh
        nrm = norm_rows(values, wide(gains[u, 0]))
        normed[i] = nrm
        mask = jnp.concatenate([maskv[i, 0], maskv[i, 1]], axis=1)[0:1]
        for h in range(4):
            val = nn(wproj[u, 0, h * 64 : h * 64 + 64], nrm)
            gat = nn(wproj[u, 1, h * 64 : h * 64 + 64], nrm)
            y = (val * sigmoid(gat) * mask).astype(BF16)
            for ih in range(2):
                asend[u, h * 4 : h * 4 + 4, q, kh, ih] = y[:, ih * 128 : ih * 128 + 128].reshape(4, 16, 128)

    def send_cols(u, q):
        def one(n):
            s = col_peer(n)
            remote(asend.at[u, s, q], arecv.at[u, c, q], u, COLS_OUT, q, r, s).start()

        loop(16, one, 1)
        arecv[u, c, q] = asend[u, c, q]

    def gates(u):
        def one(i):
            gate[i] = sigmoid(nn(wg[u], normed[i]))

        loop(9, one)

    def fill_perm():
        row = lax.broadcasted_iota(jnp.int32, (128, 128), 0)
        col = lax.broadcasted_iota(jnp.int32, (128, 128), 1)
        same = (row & 15) == (col & 15)

        def one(n):
            p = n // 8
            g = n % 8
            hit = same & ((row >> 4) == g) & ((col >> 4) == p)
            perm[g, pl.ds(pl.multiple_of(p * 128, 128), 128), :] = hit.astype(F32).astype(BF16)

        loop(64, one)

    def regroup_out(u, q):
        wait_bytes(arecv.at[u, pl.ds(0, 15), q], recv_sem.at[u, COLS_OUT, q])
        x = jnp.concatenate([arecv[u, 2 * p : 2 * p + 2, q].reshape(192, 128) for p in range(8)], axis=1)

        def one(t):
            y = nn(x, jnp.concatenate([perm[2 * t], perm[2 * t + 1]], axis=1))
            for hh in range(2):
                part = y[:, hh * 128 : hh * 128 + 128].reshape(2, 3, 2, 2, 8, 128)
                for ch in range(2):
                    for kh in range(3):
                        for ih in range(2):
                            for lr in range(2):
                                stage[lr, ch * 3 + kh, pl.ds(ih * 8 + 2 * t + hh, 8, stride=16), :] = part[ch, kh, ih, lr]

        loop(4, one)

        def pack(d):
            bsend[u, q, d] = stage[:, :, pl.ds(pl.multiple_of(d * 16, 16), 16), :].astype(BF16)

        loop(8, pack)

        def one_send(n):
            peer = row_peer(n)
            remote(bsend.at[u, q, peer], brecv.at[u, q, rb], u, ROWS_OUT, q, peer * 2 + core, c).start()

        loop(8, one_send, 1)
        brecv[u, q, rb] = bsend[u, q, rb]

    def pair_copies(u, q):
        other = rb * 2 + 1 - core
        copies = [remote(brecv.at[u, q, :, 1], rpair.at[u, q], u, PAIR_RIGHT, q, other, c)]
        if u == 1:
            copies.append(
                remote(brecv.at[u, q, :, 0, pl.ds((1 - core) * 3, 3)], lpair.at[q], u, PAIR_LEFT, q, other, c)
            )
        return copies

    def exchange(u, q):
        wait_bytes(brecv.at[u, q, pl.ds(0, 7)], recv_sem.at[u, ROWS_OUT, q])
        for copy in pair_copies(u, q):
            copy.start()

    def product_out(qi):
        u = 0
        left = jnp.concatenate([brecv[u, qi, :, 0, m].reshape(128, 128) for m in range(6)], axis=1)
        for jh in range(3):
            for own in range(2):
                if own:
                    right = jnp.concatenate([brecv[u, jh, :, 1, m].reshape(128, 128) for m in range(6)], axis=1)
                    m_out = core * 3 + jh
                else:
                    right = jnp.concatenate([rpair[u, jh, :, m].reshape(128, 128) for m in range(6)], axis=1)
                    m_out = (1 - core) * 3 + jh
                cbuf[u, qi, :, m_out] = nt(left, right).astype(BF16).reshape(8, 16, 128)

    def product_in(qi):
        u = 1
        mine = brecv[u, :, :, 0, core * 3 + qi].reshape(384, 128).astype(F32).T.astype(BF16)
        theirs = lpair[:, :, qi].reshape(384, 128).astype(F32).T.astype(BF16)
        for m in range(0, 6, 2):
            right = jnp.concatenate([brecv[u, :, :, 1, m + k].reshape(384, 128) for k in range(2)], axis=1)
            extra = jnp.concatenate([rpair[u, :, :, m + k].reshape(384, 128) for k in range(2)], axis=1)
            both = (nn(mine, right) + nn(theirs, extra)).astype(BF16)
            for k in range(2):
                cbuf[u, qi, :, m + k] = both[:, k * 128 : k * 128 + 128].reshape(8, 16, 128)

    def send_products(u, qi):
        def one(n):
            peer = row_peer(n)
            remote(cbuf.at[u, qi, peer], crecv.at[u, qi, rb], u, ROWS_BACK, qi, peer * 2 + core, c).start()

        loop(8, one, 1)
        crecv[u, qi, rb] = cbuf[u, qi, rb]

    def regroup_back(u, q):
        wait_bytes(crecv.at[u, q, pl.ds(0, 7)], recv_sem.at[u, ROWS_BACK, q])

        def unpack(d):
            stage[0, :, pl.ds(pl.multiple_of(d * 16, 16), 16), :] = crecv[u, q, d].astype(F32)

        loop(8, unpack)
        columns = []
        for il in range(8):
            rows = [stage[0, m, pl.ds(ih * 8 + il, 8, stride=16), :] for m in range(6) for ih in range(2)]
            columns.append(jnp.concatenate(rows, axis=0).astype(BF16))
        x = jnp.concatenate(columns, axis=1)

        def one(t):
            y = nn(x, jnp.concatenate([perm[2 * t], perm[2 * t + 1]], axis=1)).astype(BF16)
            for hh in range(2):
                part = y[:, hh * 128 : hh * 128 + 128].reshape(2, 3, 16, 128)
                dsend[u, pl.ds(2 * (2 * t + hh), 2), q] = part

        loop(4, one)

        def one_send(n):
            s = col_peer(n)
            remote(dsend.at[u, s, q], drecv.at[u, c, q], u, COLS_BACK, q, r, s).start()

        loop(16, one_send, 1)
        drecv[u, c, q] = dsend[u, c, q]

    def finish_chunk(u, q):
        wait_bytes(drecv.at[u, pl.ds(0, 15), q], recv_sem.at[u, COLS_BACK, q])

        def one(kh):
            i = q * 3 + kh
            got = drecv[u, :, q, kh].astype(F32).reshape(16, 2, 8, 128)
            mixed = jnp.concatenate([got[:, 0].reshape(128, 128), got[:, 1].reshape(128, 128)], axis=1)
            branch = nn(wo[u], norm_rows(mixed, wide(gains[u, 1])))
            new = (load_zt(i) + gate[i] * branch).astype(BF16).astype(F32)
            if u == 0:
                for ih in range(2):
                    zt[i, ih] = new[:, ih * 128 : ih * 128 + 128]
                project(1, q, kh, new)
            else:
                for ih in range(2):
                    tile = new[:, ih * 128 : ih * 128 + 128].T.astype(BF16).reshape(8, 16, 128)
                    out_ref[pl.ds((q * 2 + ih) * 8, 8), pl.ds(pl.multiple_of(kh * 16, 16), 16), :] = tile

        loop(3, one)

    def first(q):
        loop(3, lambda kh: project(0, q, kh, load_zt(q * 3 + kh)))

    first(0)
    pl.semaphore_wait(barrier, 23)
    send_cols(0, 0)
    for q in (1, 2):
        first(q)
        send_cols(0, q)
    fill_perm()
    for u in range(2):
        gates(u)
        regroup_out(u, 0)

        def middle(q):
            regroup_out(u, q)
            exchange(u, q - 1)

        loop(3, middle, 1)
        exchange(u, 2)
        for q in range(3):
            for copy in pair_copies(u, q):
                copy.wait_recv()

        def products(qi):
            (product_out if u == 0 else product_in)(qi)
            send_products(u, qi)

        loop(3, products)
        loop(3, lambda q: regroup_back(u, q))

        def close(q):
            finish_chunk(u, q)
            if u == 0:
                send_cols(1, q)

        loop(3, close)

    for u in range(2):

        def drain(q):
            wait_bytes(asend.at[u, pl.ds(0, 15), q], send_sem.at[u, COLS_OUT, q])
            wait_bytes(bsend.at[u, q, pl.ds(0, 7)], send_sem.at[u, ROWS_OUT, q])
            for copy in pair_copies(u, q):
                copy.wait_send()
            wait_bytes(cbuf.at[u, q, pl.ds(0, 7)], send_sem.at[u, ROWS_BACK, q])
            wait_bytes(dsend.at[u, pl.ds(0, 15), q], send_sem.at[u, COLS_BACK, q])

        loop(3, drain)


def body(pair_state, residue_mask, weight_in, weight_gate, weight_out, gain_in, gain_out):
    vmem = pl.BlockSpec(memory_space=pltpu.VMEM)
    weights = weight_in.transpose(0, 2, 1, 3)
    mask = residue_mask.reshape(1, 768)
    return pl.pallas_call(
        kernel,
        out_shape=jax.ShapeDtypeStruct((48, 48, 128), BF16),
        in_specs=[vmem] * 7,
        out_specs=vmem,
        scratch_shapes=[
            pltpu.VMEM((8, 1024, 128), BF16),
            pltpu.VMEM((9, 2, 128, 128), F32),
            pltpu.VMEM((9, 128, 256), BF16),
            pltpu.VMEM((9, 128, 256), F32),
            pltpu.VMEM((9, 2, 8, 128), F32),
            pltpu.VMEM((2, 2, 256, 128), BF16),
            pltpu.VMEM((2, 128, 128), BF16),
            pltpu.VMEM((2, 128, 128), BF16),
            pltpu.VMEM((2, 2, 128, 128), F32),
            pltpu.VMEM((2, 16, 3, 3, 2, 16, 128), BF16),
            pltpu.VMEM((2, 16, 3, 3, 2, 16, 128), BF16),
            pltpu.VMEM((2, 3, 8, 2, 6, 16, 128), BF16),
            pltpu.VMEM((2, 3, 8, 2, 6, 16, 128), BF16),
            pltpu.VMEM((2, 3, 8, 6, 16, 128), BF16),
            pltpu.VMEM((3, 8, 3, 16, 128), BF16),
            pltpu.VMEM((2, 3, 8, 6, 16, 128), BF16),
            pltpu.VMEM((2, 3, 8, 6, 16, 128), BF16),
            pltpu.VMEM((2, 16, 3, 3, 16, 128), BF16),
            pltpu.VMEM((2, 16, 3, 3, 16, 128), BF16),
            pltpu.VMEM((2, 6, 128, 128), F32),
            pltpu.SemaphoreType.DMA((2, 6, 3)),
            pltpu.SemaphoreType.DMA((2, 6, 3)),
        ],
        compiler_params=pltpu.CompilerParams(
            collective_id=0, has_side_effects=True, vmem_limit_bytes=48 * 1024 * 1024
        ),
        name="triangle",
    )(pair_state, mask, weights, weight_gate, weight_out, gain_in, gain_out)


def solution(mesh):
    return jax.shard_map(
        body,
        mesh=mesh,
        in_specs=(P("row", "col", None), P(), P(), P(), P(), P(), P()),
        out_specs=P("row", "col", None),
        check_vma=False,
    )
```

```python
import jax
import jax.numpy as jnp
from jax import lax
from jax.experimental import pallas as pl
from jax.experimental.pallas import tpu as pltpu
from jax.sharding import PartitionSpec as P

MESH = pl.DeviceIdType.MESH
F32 = jnp.float32
BF16 = jnp.bfloat16
EPS = 1e-5
COLS_OUT, ROWS_OUT, PAIR, ROWS_BACK, COLS_BACK = range(5)
BLOCKS = ((0, 0), (0, 1), (1, 0), (1, 1), (0, 2), (1, 2), (2, 0), (2, 1), (2, 2))
WAVES = ((0, 1), (1, 4), (4, 6), (6, 7), (7, 9))


def sigmoid(x):
    return 0.5 * jnp.tanh(0.5 * x) + 0.5


def norm_rows(values, gain):
    mean = jnp.sum(values, axis=0, keepdims=True) * (1.0 / 128.0)
    centered = values - mean
    var = jnp.sum(centered * centered, axis=0, keepdims=True) * (1.0 / 128.0)
    return (centered * lax.rsqrt(var + EPS) * gain).astype(BF16)


def nn(a, b):
    return lax.dot_general(a, b, (((1,), (0,)), ((), ())), preferred_element_type=F32)


def nt(a, b):
    return lax.dot_general(a, b, (((1,), (1,)), ((), ())), preferred_element_type=F32)


def tn(a, b):
    return lax.dot_general(a, b, (((0,), (0,)), ((), ())), preferred_element_type=F32)


def loop(n, body, start=0):
    def step(i, carry):
        body(i)
        return carry

    lax.fori_loop(start, n, step, 0)


def wait_bytes(ref, sem):
    pltpu.make_async_copy(ref, ref, sem).wait()


def kernel(
    x_ref, mask_ref, win_ref, wgate_ref, wout_ref, gin_ref, gout_ref, out_ref,
    perm, zt, normed, gate, maskv, wproj, wg, wo, gains,
    asend, arecv, bsend, brecv, rpair, lpair, lturn, cbuf, crecv, dsend, drecv,
    stage, stage_back, send_sem, recv_sem,
):
    r = lax.axis_index("row")
    c = lax.axis_index("col")
    core = r % 2
    rb = r // 2
    z = c % 8
    xl = c // 8

    def col_peer(n):
        hop = n // 2
        away = (hop + 1) // 2 * (1 - 2 * (hop % 2))
        return (xl + n % 2) % 2 * 8 + (z + away + 8) % 8

    def row_peer(n):
        return (rb // 2 + n // 2) % 4 * 2 + (rb + n) % 2

    barrier = pltpu.get_barrier_semaphore()

    def greet(row, col):
        pl.semaphore_signal(barrier, inc=1, device_id=(row, col), device_id_type=MESH)

    loop(16, lambda n: greet(r, col_peer(n)), 1)
    loop(8, lambda n: greet(row_peer(n) * 2 + core, c), 1)
    greet(rb * 2 + 1 - core, c)

    def remote(src, dst, u, phase, q, row, col):
        return pltpu.make_async_remote_copy(
            src_ref=src, dst_ref=dst,
            send_sem=send_sem.at[u, phase, q], recv_sem=recv_sem.at[u, phase, q],
            device_id=(row, col), device_id_type=MESH,
        )

    for u in range(2):
        for t in range(4):
            wproj[u, t] = win_ref[u, t].astype(F32).T.astype(BF16)
        wg[u] = wgate_ref[u].astype(F32).T.astype(BF16)
        wo[u] = wout_ref[u].astype(F32).T.astype(BF16)
        gains[u, 0] = jnp.broadcast_to(gin_ref[u : u + 1, :], (128, 128)).T
        gains[u, 1] = jnp.broadcast_to(gout_ref[u : u + 1, :], (128, 128)).T

    mask_row = jnp.broadcast_to(mask_ref[...].astype(F32), (8, 768)).astype(BF16)
    place = lax.broadcasted_iota(jnp.int32, (768, 128), 0)
    lane = lax.broadcasted_iota(jnp.int32, (768, 128), 1)
    col_masks = [
        nn(mask_row, (place == c * 48 + kh * 16 + (lane & 15)).astype(F32).astype(BF16)) for kh in range(3)
    ]

    def fill_masks(ihg):
        rows = nn(mask_row, (place == r * 48 + ihg * 8 + (lane >> 4)).astype(F32).astype(BF16))
        for kh in range(3):
            maskv[ihg // 2 * 3 + kh, ihg % 2] = rows * col_masks[kh]

    loop(6, fill_masks)

    def load_tile(ihg):
        for kh in range(3):
            block = x_ref[pl.ds(ihg * 8, 8), kh * 16 : kh * 16 + 16, :].reshape(128, 128)
            zt[ihg // 2 * 3 + kh, ihg % 2] = block.astype(F32).T

    loop(6, load_tile)

    def load_zt(i):
        return jnp.concatenate([zt[i, 0], zt[i, 1]], axis=1)

    def wide(block):
        return jnp.concatenate([block, block], axis=1)

    def project(u, q, kh, values):
        i = q * 3 + kh
        nrm = norm_rows(values, wide(gains[u, 0]))
        normed[i] = nrm
        mask = jnp.concatenate([maskv[i, 0], maskv[i, 1]], axis=1)[0:1]
        chunk, inner = (q, kh) if u == 0 else (kh, q)
        for side in (1, 0):
            for h in range(2):
                val = nn(wproj[u, 2 * side, h * 64 : h * 64 + 64], nrm)
                gat = nn(wproj[u, 2 * side + 1, h * 64 : h * 64 + 64], nrm)
                y = (val * sigmoid(gat) * mask).reshape(8, 8, 256)
                y = jnp.concatenate([y[:, :, :128], y[:, :, 128:]], axis=1).astype(BF16)
                asend[u, side, chunk, h * 8 : h * 8 + 8, inner] = y

    def send_cols(u, chunk):
        for side in (1, 0):
            h = 2 * chunk + 1 - side

            def one(n):
                s = col_peer(n)
                remote(asend.at[u, side, chunk, s], arecv.at[u, side, chunk, c], u, COLS_OUT, h, r, s).start()

            loop(16, one, 1)
            arecv[u, side, chunk, c] = asend[u, side, chunk, c]

    def gates(u):
        def one(i):
            gate[i] = sigmoid(nn(wg[u], normed[i]))

        loop(9, one)

    def fill_perm():
        row = lax.broadcasted_iota(jnp.int32, (128, 128), 0)
        col = lax.broadcasted_iota(jnp.int32, (128, 128), 1)
        same = (row & 15) == (col & 15)

        def one(n):
            p = n // 8
            g = n % 8
            hit = same & ((row >> 4) == g) & ((col >> 4) == p)
            perm[g, pl.ds(pl.multiple_of(p * 128, 128), 128), :] = hit.astype(F32).astype(BF16)

        loop(64, one)

    def regroup_out(u, h):
        side, chunk = 1 - h % 2, h // 2
        wait_bytes(arecv.at[u, side, chunk, pl.ds(0, 15)], recv_sem.at[u, COLS_OUT, h])
        x = jnp.concatenate(
            [arecv[u, side, chunk, 2 * p : 2 * p + 2].reshape(96, 128) for p in range(8)], axis=1
        )

        def one(t):
            y = nn(x, jnp.concatenate([perm[2 * t], perm[2 * t + 1]], axis=1))
            for hh in range(2):
                part = y[:, hh * 128 : hh * 128 + 128].reshape(6, 2, 8, 128)
                for m in range(6):
                    for ih in range(2):
                        stage[m, pl.ds(ih * 8 + 2 * t + hh, 8, stride=16), :] = part[m, ih]

        loop(4, one)

        def pack(d):
            bsend[u, side, chunk, d] = stage[:, pl.ds(pl.multiple_of(d * 16, 16), 16), :].astype(BF16)

        loop(8, pack)

        def one_send(n):
            peer = row_peer(n)
            remote(
                bsend.at[u, side, chunk, peer], brecv.at[u, side, chunk, rb], u, ROWS_OUT, h, peer * 2 + core, c
            ).start()

        loop(8, one_send, 1)
        brecv[u, side, chunk, rb] = bsend[u, side, chunk, rb]

    def pair_copy(u, h):
        side, chunk = 1 - h % 2, h // 2
        other = rb * 2 + 1 - core
        if side == 1:
            return remote(brecv.at[u, 1, chunk], rpair.at[u, chunk], u, PAIR, h, other, c)
        return remote(
            brecv.at[u, 0, chunk, :, pl.ds((1 - core) * 3, 3)], lpair.at[chunk], u, PAIR, h, other, c
        )

    def exchange(u, h):
        side, chunk = 1 - h % 2, h // 2
        wait_bytes(brecv.at[u, side, chunk, pl.ds(0, 7)], recv_sem.at[u, ROWS_OUT, h])
        if side == 1 or u == 1:
            pair_copy(u, h).start()

    def exchanged(u, h):
        if h % 2 == 0 or u == 1:
            pair_copy(u, h).wait_recv()
        if h % 2 == 1 and u == 1:
            chunk = h // 2
            mine = brecv[u, 0, chunk, :, pl.ds(core * 3, 3)].reshape(384, 128)
            theirs = lpair[chunk].reshape(384, 128)
            lturn[chunk, 0] = mine.astype(F32).T.astype(BF16)
            lturn[chunk, 1] = theirs.astype(F32).T.astype(BF16)

    def product(u, n):
        qi, jh = BLOCKS[n]
        if u == 0:
            left = jnp.concatenate([brecv[u, 0, qi, :, m].reshape(128, 128) for m in range(6)], axis=1)
            mine = jnp.concatenate([brecv[u, 1, jh, :, m].reshape(128, 128) for m in range(6)], axis=1)
            theirs = jnp.concatenate([rpair[u, jh, :, m].reshape(128, 128) for m in range(6)], axis=1)
            both = nt(left, jnp.concatenate([mine, theirs], axis=0)).astype(BF16)
            places = (core, 1 - core)
        else:
            mine = jnp.concatenate(
                [brecv[u, 1, jh, :, 3 * k : 3 * k + 3].reshape(384, 128) for k in range(2)], axis=1
            )
            theirs = jnp.concatenate(
                [rpair[u, jh, :, 3 * k : 3 * k + 3].reshape(384, 128) for k in range(2)], axis=1
            )
            both = (nn(lturn[qi, 0], mine) + nn(lturn[qi, 1], theirs)).astype(BF16)
            places = (0, 1)
        for k in range(2):
            cbuf[u, :, n, places[k]] = both[:, k * 128 : k * 128 + 128].reshape(8, 16, 128)

    def products(u, w):
        begin, end = WAVES[w]
        for n in range(begin, end):
            product(u, n)
        span = pl.ds(begin, end - begin)

        def one(n):
            peer = row_peer(n)
            remote(
                cbuf.at[u, peer, span], crecv.at[u, rb, span], u, ROWS_BACK, w, peer * 2 + core, c
            ).start()

        loop(8, one, 1)
        crecv[u, rb, span] = cbuf[u, rb, span]

    def regroup_back(u, w):
        begin, end = WAVES[w]
        size = end - begin
        span = pl.ds(begin, size)
        wait_bytes(crecv.at[u, pl.ds(0, 7), span], recv_sem.at[u, ROWS_BACK, w])

        def unpack(d):
            stage_back[0:size, :, pl.ds(pl.multiple_of(d * 16, 16), 16), :] = crecv[u, d, span].astype(F32)

        loop(8, unpack)
        columns = []
        for il in range(8):
            rows = [
                stage_back[n, ch, pl.ds(ih * 8 + il, 8, stride=16), :]
                for n in range(size) for ch in range(2) for ih in range(2)
            ]
            columns.append(jnp.concatenate(rows, axis=0).astype(BF16))
        x = jnp.concatenate(columns, axis=1)

        def one(t):
            y = nn(x, jnp.concatenate([perm[2 * t], perm[2 * t + 1]], axis=1)).astype(BF16)
            for hh in range(2):
                part = y[:, hh * 128 : hh * 128 + 128].reshape(size, 2, 16, 128)
                for ch in range(2):
                    dsend[u, 2 * (2 * t + hh) + ch, span] = part[:, ch]

        loop(4, one)

        def one_send(n):
            s = col_peer(n)
            remote(dsend.at[u, s, span], drecv.at[u, c, span], u, COLS_BACK, w, r, s).start()

        loop(16, one_send, 1)
        drecv[u, c, span] = dsend[u, c, span]

    def arrive_back(u, w):
        begin, end = WAVES[w]
        wait_bytes(drecv.at[u, pl.ds(0, 15), pl.ds(begin, end - begin)], recv_sem.at[u, COLS_BACK, w])

    def finish(u, n):
        q, kh = BLOCKS[n]
        i = q * 3 + kh
        got = drecv[u, :, n].astype(F32).reshape(16, 2, 8, 128)
        mixed = jnp.concatenate([got[:, 0].reshape(128, 128), got[:, 1].reshape(128, 128)], axis=1)
        branch = nn(wo[u], norm_rows(mixed, wide(gains[u, 1])))
        new = (load_zt(i) + gate[i] * branch).astype(BF16).astype(F32)
        for ih in range(2):
            half = new[:, ih * 128 : ih * 128 + 128]
            if u == 0:
                zt[i, ih] = half
            else:
                rows = (q * 2 + ih) * 8
                out_ref[rows : rows + 8, kh * 16 : kh * 16 + 16, :] = half.T.astype(BF16).reshape(8, 16, 128)
        if u == 0:
            project(1, q, kh, new)

    def first(q):
        loop(3, lambda kh: project(0, q, kh, load_zt(q * 3 + kh)))

    first(0)
    pl.semaphore_wait(barrier, 23)
    send_cols(0, 0)
    for q in (1, 2):
        first(q)
        send_cols(0, q)
    fill_perm()
    for u in range(2):
        gates(u)
        regroup_out(u, 0)
        regroup_out(u, 1)
        exchange(u, 0)
        regroup_out(u, 2)
        exchange(u, 1)
        exchanged(u, 0)
        exchanged(u, 1)
        products(u, 0)
        regroup_out(u, 3)
        exchange(u, 2)
        regroup_out(u, 4)
        exchange(u, 3)
        exchanged(u, 2)
        exchanged(u, 3)
        products(u, 1)
        regroup_back(u, 0)
        regroup_out(u, 5)
        exchange(u, 4)
        regroup_back(u, 1)
        exchanged(u, 4)
        products(u, 2)
        exchange(u, 5)
        exchanged(u, 5)
        products(u, 3)
        products(u, 4)
        regroup_back(u, 2)
        arrive_back(u, 0)
        finish(u, 0)
        arrive_back(u, 1)
        for n in (1, 2, 3):
            finish(u, n)
        regroup_back(u, 3)
        regroup_back(u, 4)
        arrive_back(u, 2)
        for n in (4, 5):
            finish(u, n)
        arrive_back(u, 3)
        finish(u, 6)
        if u == 0:
            send_cols(1, 0)
        arrive_back(u, 4)
        for n in (7, 8):
            finish(u, n)
            if u == 0:
                send_cols(1, n - 6)

    for u in range(2):
        for h in range(6):
            side, chunk = 1 - h % 2, h // 2
            wait_bytes(asend.at[u, side, chunk, pl.ds(0, 15)], send_sem.at[u, COLS_OUT, h])
            wait_bytes(bsend.at[u, side, chunk, pl.ds(0, 7)], send_sem.at[u, ROWS_OUT, h])
            if side == 1 or u == 1:
                pair_copy(u, h).wait_send()
        for w, (begin, end) in enumerate(WAVES):
            span = pl.ds(begin, end - begin)
            wait_bytes(cbuf.at[u, pl.ds(0, 7), span], send_sem.at[u, ROWS_BACK, w])
            wait_bytes(dsend.at[u, pl.ds(0, 15), span], send_sem.at[u, COLS_BACK, w])


def body(pair_state, residue_mask, weight_in, weight_gate, weight_out, gain_in, gain_out):
    vmem = pl.BlockSpec(memory_space=pltpu.VMEM)
    weights = weight_in.transpose(0, 2, 1, 3)
    mask = residue_mask.reshape(1, 768)
    return pl.pallas_call(
        kernel,
        out_shape=jax.ShapeDtypeStruct((48, 48, 128), BF16),
        in_specs=[vmem] * 7,
        out_specs=vmem,
        scratch_shapes=[
            pltpu.VMEM((8, 1024, 128), BF16),
            pltpu.VMEM((9, 2, 128, 128), F32),
            pltpu.VMEM((9, 128, 256), BF16),
            pltpu.VMEM((9, 128, 256), F32),
            pltpu.VMEM((9, 2, 8, 128), F32),
            pltpu.VMEM((2, 4, 128, 128), BF16),
            pltpu.VMEM((2, 128, 128), BF16),
            pltpu.VMEM((2, 128, 128), BF16),
            pltpu.VMEM((2, 2, 128, 128), F32),
            pltpu.VMEM((2, 2, 3, 16, 3, 16, 128), BF16),
            pltpu.VMEM((2, 2, 3, 16, 3, 16, 128), BF16),
            pltpu.VMEM((2, 2, 3, 8, 6, 16, 128), BF16),
            pltpu.VMEM((2, 2, 3, 8, 6, 16, 128), BF16),
            pltpu.VMEM((2, 3, 8, 6, 16, 128), BF16),
            pltpu.VMEM((3, 8, 3, 16, 128), BF16),
            pltpu.VMEM((3, 2, 128, 384), BF16),
            pltpu.VMEM((2, 8, 9, 2, 16, 128), BF16),
            pltpu.VMEM((2, 8, 9, 2, 16, 128), BF16),
            pltpu.VMEM((2, 16, 9, 16, 128), BF16),
            pltpu.VMEM((2, 16, 9, 16, 128), BF16),
            pltpu.VMEM((6, 128, 128), F32),
            pltpu.VMEM((3, 2, 128, 128), F32),
            pltpu.SemaphoreType.DMA((2, 5, 6)),
            pltpu.SemaphoreType.DMA((2, 5, 6)),
        ],
        compiler_params=pltpu.CompilerParams(
            collective_id=0, has_side_effects=True, vmem_limit_bytes=48 * 1024 * 1024
        ),
        name="triangle",
    )(pair_state, mask, weights, weight_gate, weight_out, gain_in, gain_out)


def solution(mesh):
    return jax.shard_map(
        body,
        mesh=mesh,
        in_specs=(P("row", "col", None), P(), P(), P(), P(), P(), P()),
        out_specs=P("row", "col", None),
        check_vma=False,
    )
```

```python
import jax
import jax.numpy as jnp
from jax import lax
from jax.experimental import pallas as pl
from jax.experimental.pallas import tpu as pltpu
from jax.sharding import PartitionSpec as P

MESH = pl.DeviceIdType.MESH
F32 = jnp.float32
BF16 = jnp.bfloat16
EPS = 1e-5
COLS_OUT, ROWS_OUT, PAIR, ROWS_BACK, COLS_BACK, RIGHT_ROWS, RIGHT_COLS = range(7)
AHEAD = 2
BLOCKS = ((0, 0), (1, 0), (2, 0), (0, 1), (1, 1), (2, 1), (0, 2), (1, 2), (2, 2))
WAVES = ((0, 2), (2, 3), (3, 6), (6, 9))
PLAN = (
    ("out", 0), ("left", 2), ("mid", 0), ("out", 1), ("mid", 1), ("out", 2), ("take", 0), ("take", 1), ("in", 0), ("mid", 2), ("gates", 0), ("turn", 0), ("turn", 1), ("take", 2), ("pair", 0), ("product", 0), ("turn", 2), ("product", 1), ("in", 1), ("back", 0), ("back", 1), ("pair", 1), ("product", 2), ("in", 2), ("land", 0), ("finish", 0), ("finish", 1), ("pair", 2), ("product", 3), ("back", 2), ("land", 1), ("finish", 2), ("next", 0), ("back", 3), ("land", 2), ("finish", 3), ("finish", 4), ("finish", 5), ("next", 1), ("land", 3), ("finish", 6), ("finish", 7), ("finish", 8), ("next", 2),
)


def sigmoid(x):
    return 0.5 * jnp.tanh(0.5 * x) + 0.5


def norm_rows(values, gain):
    mean = jnp.sum(values, axis=0, keepdims=True) * (1.0 / 128.0)
    centered = values - mean
    var = jnp.sum(centered * centered, axis=0, keepdims=True) * (1.0 / 128.0)
    return (centered * lax.rsqrt(var + EPS) * gain).astype(BF16)


def nn(a, b):
    return lax.dot_general(a, b, (((1,), (0,)), ((), ())), preferred_element_type=F32)


def nt(a, b):
    return lax.dot_general(a, b, (((1,), (1,)), ((), ())), preferred_element_type=F32)


def tn(a, b):
    return lax.dot_general(a, b, (((0,), (0,)), ((), ())), preferred_element_type=F32)


def swap_lanes(blocks):
    blocks = list(blocks)
    lane = lax.broadcasted_iota(jnp.int32, blocks[0].shape, 1)
    for k in (4, 2, 1):
        low = (lane & (16 * k)) == 0
        for p in range(8):
            if p & k == 0:
                a, b = blocks[p], blocks[p | k]
                blocks[p] = jnp.where(low, a, pltpu.roll(b, 16 * k, 1))
                blocks[p | k] = jnp.where(low, pltpu.roll(a, 128 - 16 * k, 1), b)
    return blocks


def loop(n, body, start=0):
    def step(i, carry):
        body(i)
        return carry

    lax.fori_loop(start, n, step, 0)


def wait_bytes(ref, sem):
    pltpu.make_async_copy(ref, ref, sem).wait()


def kernel(
    x_ref, mask_ref, win_ref, wgate_ref, wout_ref, gin_ref, gout_ref, out_ref,
    xbuf, zt, normed, gate, maskv, wproj, wg, wo, gains,
    asend, arecv, bsend, brecv, rsend, rmid, tsend, trecv, rmat, rpair, lpair, lturn, cbuf, crecv, dsend, drecv,
    stage, stage_mid, stage_back, tile_sem, send_sem, recv_sem,
):
    r = lax.axis_index("row")
    c = lax.axis_index("col")
    core = r % 2
    rb = r // 2
    z = c % 8
    xl = c // 8

    zs = [(z + d) % 8 for d in range(8)]
    xs = [xl * 8, (1 - xl) * 8]
    ys = [(rb // 2 + d) % 4 * 2 for d in range(4)]
    hs = [rb % 2, 1 - rb % 2]

    def col_peer(n):
        hop = n // 2
        away = (hop + 1) // 2 * (1 - 2 * (hop % 2))
        return xs[n % 2] + zs[away % 8]

    def row_peer(n):
        return ys[n // 2] + hs[n % 2]

    def unrolled(n, body):
        for i in range(1, n):
            body(i)

    barrier = pltpu.get_barrier_semaphore()

    def greet(row, col):
        pl.semaphore_signal(barrier, inc=1, device_id=(row, col), device_id_type=MESH)

    unrolled(16, lambda n: greet(r, col_peer(n)))
    unrolled(8, lambda n: greet(row_peer(n) * 2 + core, c))
    greet(rb * 2 + 1 - core, c)

    def remote(src, dst, u, phase, q, row, col):
        return pltpu.make_async_remote_copy(
            src_ref=src, dst_ref=dst,
            send_sem=send_sem.at[u, phase, q], recv_sem=recv_sem.at[u, phase, q],
            device_id=(row, col), device_id_type=MESH,
        )

    tile_copies = [
        pltpu.make_async_copy(x_ref.at[pl.ds(q * 16, 16)], xbuf.at[pl.ds(q * 16, 16)], tile_sem.at[q]) for q in range(3)
    ]
    for copy in tile_copies:
        copy.start()

    def prepare_in(u):
        for t in range(4):
            turned = win_ref[u, t].astype(F32).T
            if t < 2:
                wproj[u, t] = turned.astype(BF16)
            else:
                stage[t] = turned
                for g in range(8):
                    wproj[u, t, g * 16 : g * 16 + 16] = stage[t, pl.ds(g, 16, stride=8), :].astype(BF16)
        gains[u, 0] = jnp.broadcast_to(gin_ref[u : u + 1, :], (128, 128)).T

    def prepare_rest(u):
        wg[u] = wgate_ref[u].astype(F32).T.astype(BF16)
        wo[u] = wout_ref[u].astype(F32).T.astype(BF16)
        gains[u, 1] = jnp.broadcast_to(gout_ref[u : u + 1, :], (128, 128)).T

    prepare_in(0)
    mask_row = jnp.broadcast_to(mask_ref[...].astype(F32)[None, :], (8, 768))
    row_part = pltpu.roll(mask_row, (768 - r * 48) % 768, 1)[:, :128].astype(BF16)
    col_part = pltpu.roll(mask_row, (768 - c * 48) % 768, 1)[:, :128].astype(BF16)
    place = lax.broadcasted_iota(jnp.int32, (128, 128), 0)
    lane = lax.broadcasted_iota(jnp.int32, (128, 128), 1)
    col_masks = [nn(col_part, (place == kh * 16 + (lane & 15)).astype(F32).astype(BF16)) for kh in range(3)]

    def load_rows(q):
        tile_copies[q].wait()
        for ih in range(2):
            ihg = q * 2 + ih
            rows = nn(row_part, (place == ihg * 8 + (lane >> 4)).astype(F32).astype(BF16))
            for kh in range(3):
                maskv[q * 3 + kh, ih] = rows * col_masks[kh]
                block = xbuf[ihg * 8 : ihg * 8 + 8, kh * 16 : kh * 16 + 16, :].reshape(128, 128)
                zt[q * 3 + kh, ih] = block.astype(F32).T

    def load_zt(i):
        return jnp.concatenate([zt[i, 0], zt[i, 1]], axis=1)

    def wide(block):
        return jnp.concatenate([block, block], axis=1)

    def project(u, q, kh, values):
        i = q * 3 + kh
        nrm = norm_rows(values, wide(gains[u, 0]))
        normed[i] = nrm
        mask = jnp.concatenate([maskv[i, 0], maskv[i, 1]], axis=1)[0:1]
        chunk, inner = (q, kh) if u == 0 else (kh, q)
        for side in (1, 0):
            for h in range(2):
                val = nn(wproj[u, 2 * side, h * 64 : h * 64 + 64], nrm)
                gat = nn(wproj[u, 2 * side + 1, h * 64 : h * 64 + 64], nrm)
                y = val * sigmoid(gat) * mask
                if side == 0:
                    y = y.reshape(8, 8, 256)
                    y = jnp.concatenate([y[:, :, :128], y[:, :, 128:]], axis=1).astype(BF16)
                    asend[u, chunk, h * 8 : h * 8 + 8, inner] = y
                else:
                    for ih in range(2):
                        part = y[:, ih * 128 : ih * 128 + 128].astype(BF16).reshape(4, 16, 128)
                        rsend[u, chunk, h * 4 : h * 4 + 4, inner, ih] = part

    def send_left(u, chunk):
        def one(n):
            s = col_peer(n)
            remote(asend.at[u, chunk, s], arecv.at[u, chunk, c], u, COLS_OUT, chunk, r, s).start()

        unrolled(16, one)
        arecv[u, chunk, c] = asend[u, chunk, c]

    def send_right(u, chunk):
        def one(n):
            peer = row_peer(n)
            remote(
                rsend.at[u, chunk, peer], rmid.at[u, chunk, rb], u, RIGHT_ROWS, chunk, peer * 2 + core, c
            ).start()

        unrolled(8, one)
        rmid[u, chunk, rb] = rsend[u, chunk, rb]

    def send_chunk(u, chunk):
        send_right(u, chunk)
        if chunk < AHEAD:
            send_left(u, chunk)

    def gates(u):
        def one(i):
            gate[i] = sigmoid(nn(wg[u], normed[i]))

        loop(9, one)

    def left_out(u, chunk):
        wait_bytes(arecv.at[u, chunk, pl.ds(0, 15)], recv_sem.at[u, COLS_OUT, chunk])

        def one(m):
            ch, inner = m // 3, m % 3
            parts = swap_lanes([arecv[u, chunk, 2 * p + ch, inner].astype(F32) for p in range(8)])
            for il in range(8):
                for ih in range(2):
                    stage[m, pl.ds(ih * 8 + il, 8, stride=16), :] = parts[il][ih * 8 : ih * 8 + 8]

        for m in range(6):
            one(m)

        def pack(d):
            bsend[u, chunk, d] = stage[:, d * 16 : d * 16 + 16, :].astype(BF16)

        for d in range(8):
            pack(d)

        def one_send(n):
            peer = row_peer(n)
            remote(
                bsend.at[u, chunk, peer], brecv.at[u, chunk, rb], u, ROWS_OUT, chunk, peer * 2 + core, c
            ).start()

        unrolled(8, one_send)
        brecv[u, chunk, rb] = bsend[u, chunk, rb]

    def left_copy(chunk):
        part = brecv.at[1, chunk, :, pl.ds((1 - core) * 3, 3)]
        return remote(part, lpair.at[chunk], 1, PAIR, 3 + chunk, rb * 2 + 1 - core, c)

    def left_take(u, chunk):
        wait_bytes(brecv.at[u, chunk, pl.ds(0, 7)], recv_sem.at[u, ROWS_OUT, chunk])
        if u == 1:
            left_copy(chunk).start()

    def left_turn(u, chunk):
        if u == 1:
            left_copy(chunk).wait_recv()
            for k in range(3):
                mine = brecv[u, chunk, :, core * 3 + k].reshape(128, 128)
                theirs = lpair[chunk, :, k].reshape(128, 128)
                lturn[chunk, 0, :, k * 128 : k * 128 + 128] = mine.astype(F32).T.astype(BF16)
                lturn[chunk, 1, :, k * 128 : k * 128 + 128] = theirs.astype(F32).T.astype(BF16)

    def right_mid(u, chunk):
        wait_bytes(rmid.at[u, chunk, pl.ds(0, 7)], recv_sem.at[u, RIGHT_ROWS, chunk])

        def one(inner):
            for g in range(8):
                for ih in range(2):
                    at = (g * 2 + ih) * 16
                    stage_mid[inner, at : at + 16, :] = rmid[u, chunk, g, inner, ih].astype(F32)
            for s in range(16):
                tsend[u, chunk, s, inner] = stage_mid[inner, pl.ds(s, 16, stride=16), :].astype(BF16)

        for inner in range(3):
            one(inner)

        def one_send(n):
            s = col_peer(n)
            remote(tsend.at[u, chunk, s], trecv.at[u, chunk, c], u, RIGHT_COLS, chunk, r, s).start()

        unrolled(16, one_send)
        trecv[u, chunk, c] = tsend[u, chunk, c]

    def right_copy(u, chunk):
        return remote(rmat.at[u, chunk], rpair.at[u, chunk], u, PAIR, chunk, rb * 2 + 1 - core, c)

    def right_in(u, chunk):
        wait_bytes(trecv.at[u, chunk, pl.ds(0, 15)], recv_sem.at[u, RIGHT_COLS, chunk])

        def one(m):
            ch, inner = m // 3, m % 3
            parts = swap_lanes([trecv[u, chunk, 2 * p + ch, inner].astype(F32) for p in range(8)])
            for il in range(8):
                stage[m, pl.ds(il, 16, stride=8), :] = parts[il]
            rmat[u, chunk, m] = stage[m].astype(BF16)

        for m in range(6):
            one(m)
        right_copy(u, chunk).start()

    def product(u, n):
        qi, jh = BLOCKS[n]
        if u == 0:
            left = jnp.concatenate([brecv[u, qi, :, m].reshape(128, 128) for m in range(6)], axis=1)
            mine = jnp.concatenate([rmat[u, jh, m] for m in range(6)], axis=1)
            theirs = jnp.concatenate([rpair[u, jh, m] for m in range(6)], axis=1)
            both = nt(left, jnp.concatenate([mine, theirs], axis=0)).astype(BF16)
            places = (core, 1 - core)
        else:
            mine = jnp.concatenate(
                [rmat[u, jh, 3 * k : 3 * k + 3].reshape(384, 128) for k in range(2)], axis=1
            )
            theirs = jnp.concatenate(
                [rpair[u, jh, 3 * k : 3 * k + 3].reshape(384, 128) for k in range(2)], axis=1
            )
            both = (nn(lturn[qi, 0], mine) + nn(lturn[qi, 1], theirs)).astype(BF16)
            places = (0, 1)
        for k in range(2):
            cbuf[u, :, n, places[k]] = both[:, k * 128 : k * 128 + 128].reshape(8, 16, 128)

    def products(u, w):
        begin, end = WAVES[w]
        for n in range(begin, end):
            product(u, n)
        span = pl.ds(begin, end - begin)

        def one(n):
            peer = row_peer(n)
            remote(
                cbuf.at[u, peer, span], crecv.at[u, rb, span], u, ROWS_BACK, w, peer * 2 + core, c
            ).start()

        unrolled(8, one)
        crecv[u, rb, span] = cbuf[u, rb, span]

    def regroup_back(u, w):
        begin, end = WAVES[w]
        size = end - begin
        span = pl.ds(begin, size)
        wait_bytes(crecv.at[u, pl.ds(0, 7), span], recv_sem.at[u, ROWS_BACK, w])

        def unpack(d):
            stage_back[0:size, :, d * 16 : d * 16 + 16, :] = crecv[u, d, span].astype(F32)

        for d in range(8):
            unpack(d)

        def one(n):
            for ch in range(2):
                rows = [
                    jnp.concatenate(
                        [stage_back[n, ch, pl.ds(ih * 8 + il, 8, stride=16), :] for ih in range(2)], axis=0
                    )
                    for il in range(8)
                ]
                for p, part in enumerate(swap_lanes(rows)):
                    dsend[u, 2 * p + ch, begin + n] = part.astype(BF16)

        for n in range(size):
            one(n)

        def one_send(n):
            s = col_peer(n)
            remote(dsend.at[u, s, span], drecv.at[u, c, span], u, COLS_BACK, w, r, s).start()

        unrolled(16, one_send)
        drecv[u, c, span] = dsend[u, c, span]

    def arrive_back(u, w):
        begin, end = WAVES[w]
        wait_bytes(drecv.at[u, pl.ds(0, 15), pl.ds(begin, end - begin)], recv_sem.at[u, COLS_BACK, w])

    def finish(u, n):
        q, kh = BLOCKS[n]
        i = q * 3 + kh
        got = drecv[u, :, n].astype(F32).reshape(16, 2, 8, 128)
        mixed = jnp.concatenate([got[:, 0].reshape(128, 128), got[:, 1].reshape(128, 128)], axis=1)
        branch = nn(wo[u], norm_rows(mixed, wide(gains[u, 1])))
        new = (load_zt(i) + gate[i] * branch).astype(BF16).astype(F32)
        for ih in range(2):
            half = new[:, ih * 128 : ih * 128 + 128]
            if u == 0:
                zt[i, ih] = half
            else:
                rows = (q * 2 + ih) * 8
                out_ref[rows : rows + 8, kh * 16 : kh * 16 + 16, :] = half.T.astype(BF16).reshape(8, 16, 128)
        if u == 0:
            project(1, q, kh, new)

    def first(q):
        load_rows(q)
        loop(3, lambda kh: project(0, q, kh, load_zt(q * 3 + kh)))

    first(0)
    pl.semaphore_wait(barrier, 23)
    send_chunk(0, 0)
    for q in (1, 2):
        first(q)
        send_chunk(0, q)
    prepare_in(1)
    for u in range(2):
        prepare_rest(u)
    steps = {
        "left": send_left, "gates": lambda u, index: gates(u), "out": left_out, "take": left_take, "turn": left_turn, "mid": right_mid, "in": right_in,
        "pair": lambda u, chunk: right_copy(u, chunk).wait_recv(), "product": products, "back": regroup_back,
        "land": arrive_back, "finish": finish, "next": lambda u, chunk: send_chunk(1, chunk) if u == 0 else None,
    }
    for u in range(2):
        for step, index in PLAN:
            steps[step](u, index)

    for u in range(2):
        for chunk in range(3):
            wait_bytes(asend.at[u, chunk, pl.ds(0, 15)], send_sem.at[u, COLS_OUT, chunk])
            wait_bytes(bsend.at[u, chunk, pl.ds(0, 7)], send_sem.at[u, ROWS_OUT, chunk])
            wait_bytes(rsend.at[u, chunk, pl.ds(0, 7)], send_sem.at[u, RIGHT_ROWS, chunk])
            wait_bytes(tsend.at[u, chunk, pl.ds(0, 15)], send_sem.at[u, RIGHT_COLS, chunk])
            right_copy(u, chunk).wait_send()
            if u == 1:
                left_copy(chunk).wait_send()
        for w, (begin, end) in enumerate(WAVES):
            span = pl.ds(begin, end - begin)
            wait_bytes(cbuf.at[u, pl.ds(0, 7), span], send_sem.at[u, ROWS_BACK, w])
            wait_bytes(dsend.at[u, pl.ds(0, 15), span], send_sem.at[u, COLS_BACK, w])


def body(pair_state, residue_mask, weight_in, weight_gate, weight_out, gain_in, gain_out):
    vmem = pl.BlockSpec(memory_space=pltpu.VMEM)
    weights = weight_in.transpose(0, 2, 1, 3)
    mask = residue_mask
    return pl.pallas_call(
        kernel,
        out_shape=jax.ShapeDtypeStruct((48, 48, 128), BF16),
        in_specs=[pl.BlockSpec(memory_space=pl.ANY)] + [vmem] * 6,
        out_specs=vmem,
        scratch_shapes=[
            pltpu.VMEM((48, 48, 128), BF16),
            pltpu.VMEM((9, 2, 128, 128), F32),
            pltpu.VMEM((9, 128, 256), BF16),
            pltpu.VMEM((9, 128, 256), F32),
            pltpu.VMEM((9, 2, 8, 128), F32),
            pltpu.VMEM((2, 4, 128, 128), BF16),
            pltpu.VMEM((2, 128, 128), BF16),
            pltpu.VMEM((2, 128, 128), BF16),
            pltpu.VMEM((2, 2, 128, 128), F32),
            pltpu.VMEM((2, 3, 16, 3, 16, 128), BF16),
            pltpu.VMEM((2, 3, 16, 3, 16, 128), BF16),
            pltpu.VMEM((2, 3, 8, 6, 16, 128), BF16),
            pltpu.VMEM((2, 3, 8, 6, 16, 128), BF16),
            pltpu.VMEM((2, 3, 8, 3, 2, 16, 128), BF16),
            pltpu.VMEM((2, 3, 8, 3, 2, 16, 128), BF16),
            pltpu.VMEM((2, 3, 16, 3, 16, 128), BF16),
            pltpu.VMEM((2, 3, 16, 3, 16, 128), BF16),
            pltpu.VMEM((2, 3, 6, 128, 128), BF16),
            pltpu.VMEM((2, 3, 6, 128, 128), BF16),
            pltpu.VMEM((3, 8, 3, 16, 128), BF16),
            pltpu.VMEM((3, 2, 128, 384), BF16),
            pltpu.VMEM((2, 8, 9, 2, 16, 128), BF16),
            pltpu.VMEM((2, 8, 9, 2, 16, 128), BF16),
            pltpu.VMEM((2, 16, 9, 16, 128), BF16),
            pltpu.VMEM((2, 16, 9, 16, 128), BF16),
            pltpu.VMEM((6, 128, 128), F32),
            pltpu.VMEM((3, 256, 128), F32),
            pltpu.VMEM((3, 2, 128, 128), F32),
            pltpu.SemaphoreType.DMA((3,)),
            pltpu.SemaphoreType.DMA((2, 7, 6)),
            pltpu.SemaphoreType.DMA((2, 7, 6)),
        ],
        compiler_params=pltpu.CompilerParams(
            collective_id=0, has_side_effects=True, vmem_limit_bytes=48 * 1024 * 1024
        ),
        name="triangle",
    )(pair_state, mask, weights, weight_gate, weight_out, gain_in, gain_out)


def solution(mesh):
    return jax.shard_map(
        body,
        mesh=mesh,
        in_specs=(P("row", "col", None), P(), P(), P(), P(), P(), P()),
        out_specs=P("row", "col", None),
        check_vma=False,
    )
```

```python
import jax
import jax.numpy as jnp
from jax import lax
from jax.experimental import pallas as pl
from jax.experimental.pallas import tpu as pltpu
from jax.sharding import PartitionSpec as P

MESH = pl.DeviceIdType.MESH
F32 = jnp.float32
BF16 = jnp.bfloat16
EPS = 1e-5
COLS_OUT, ROWS_OUT, PAIR, ROWS_BACK, COLS_BACK, RIGHT_ROWS, RIGHT_COLS = range(7)
AHEAD = 2
BLOCKS = ((0, 0), (1, 0), (2, 0), (0, 1), (1, 1), (2, 1), (0, 2), (1, 2), (2, 2))
WAVES = ((0, 2), (2, 3), (3, 6), (6, 7), (7, 9))
PLAN = (
    ("out", 0), ("left", 2), ("mid", 0), ("out", 1), ("mid", 1), ("out", 2), ("take", 0), ("take", 1), ("in", 0), ("mid", 2), ("gates", 0), ("turn", 0), ("turn", 1), ("take", 2), ("pair", 0), ("product", 0), ("turn", 2), ("product", 1), ("in", 1), ("back", 0), ("back", 1), ("pair", 1), ("product", 2), ("in", 2), ("land", 0), ("finish", 0), ("finish", 1), ("pair", 2), ("product", 3), ("product", 4), ("back", 2), ("land", 1), ("finish", 2), ("next", 0), ("back", 3), ("back", 4), ("land", 2), ("finish", 3), ("finish", 4), ("finish", 5), ("next", 1), ("land", 3), ("finish", 6), ("land", 4), ("finish", 7), ("finish", 8), ("next", 2),
)


def sigmoid(x):
    return 0.5 * jnp.tanh(0.5 * x) + 0.5


def norm_rows(values, gain):
    mean = jnp.sum(values, axis=0, keepdims=True) * (1.0 / 128.0)
    centered = values - mean
    var = jnp.sum(centered * centered, axis=0, keepdims=True) * (1.0 / 128.0)
    return (centered * lax.rsqrt(var + EPS) * gain).astype(BF16)


def nn(a, b):
    return lax.dot_general(a, b, (((1,), (0,)), ((), ())), preferred_element_type=F32)


def nt(a, b):
    return lax.dot_general(a, b, (((1,), (1,)), ((), ())), preferred_element_type=F32)


def tn(a, b):
    return lax.dot_general(a, b, (((0,), (0,)), ((), ())), preferred_element_type=F32)


def swap_lanes(blocks):
    blocks = list(blocks)
    lane = lax.broadcasted_iota(jnp.int32, blocks[0].shape, 1)
    for k in (4, 2, 1):
        low = (lane & (16 * k)) == 0
        for p in range(8):
            if p & k == 0:
                a, b = blocks[p], blocks[p | k]
                blocks[p] = jnp.where(low, a, pltpu.roll(b, 16 * k, 1))
                blocks[p | k] = jnp.where(low, pltpu.roll(a, 128 - 16 * k, 1), b)
    return blocks


def loop(n, body, start=0):
    def step(i, carry):
        body(i)
        return carry

    lax.fori_loop(start, n, step, 0)


def wait_bytes(ref, sem):
    pltpu.make_async_copy(ref, ref, sem).wait()


def kernel(
    x_ref, mask_ref, win_ref, wgate_ref, wout_ref, gin_ref, gout_ref, out_ref,
    xbuf, zt, normed, gate, maskv, wproj, wg, wo, gains,
    asend, arecv, bsend, brecv, rsend, rmid, tsend, trecv, rmat, rpair, lpair, lturn, cbuf, crecv, dsend, drecv,
    stage, stage_mid, stage_back, tile_sem, send_sem, recv_sem,
):
    r = lax.axis_index("row")
    c = lax.axis_index("col")
    core = r % 2
    rb = r // 2
    z = c % 8
    xl = c // 8

    zs = [(z + d) % 8 for d in range(8)]
    xs = [xl * 8, (1 - xl) * 8]
    ys = [(rb // 2 + d) % 4 * 2 for d in range(4)]
    hs = [rb % 2, 1 - rb % 2]

    def col_peer(n):
        hop = n // 2
        away = (hop + 1) // 2 * (1 - 2 * (hop % 2))
        return xs[n % 2] + zs[away % 8]

    def row_peer(n):
        return ys[n // 2] + hs[n % 2]

    def unrolled(n, body):
        for i in range(n - 1, 0, -1):
            body(i)

    barrier = pltpu.get_barrier_semaphore()

    def greet(row, col):
        pl.semaphore_signal(barrier, inc=1, device_id=(row, col), device_id_type=MESH)

    unrolled(16, lambda n: greet(r, col_peer(n)))
    unrolled(8, lambda n: greet(row_peer(n) * 2 + core, c))
    greet(rb * 2 + 1 - core, c)

    def remote(src, dst, u, phase, q, row, col):
        return pltpu.make_async_remote_copy(
            src_ref=src, dst_ref=dst,
            send_sem=send_sem.at[u, phase, q], recv_sem=recv_sem.at[u, phase, q],
            device_id=(row, col), device_id_type=MESH,
        )

    tile_copies = [
        pltpu.make_async_copy(x_ref.at[pl.ds(q * 16, 16)], xbuf.at[pl.ds(q * 16, 16)], tile_sem.at[q]) for q in range(3)
    ]
    for copy in tile_copies:
        copy.start()

    def prepare_in(u):
        for t in range(4):
            turned = win_ref[u, t].astype(F32).T
            if t < 2:
                wproj[u, t] = turned.astype(BF16)
            else:
                stage[t] = turned
                for g in range(8):
                    wproj[u, t, g * 16 : g * 16 + 16] = stage[t, pl.ds(g, 16, stride=8), :].astype(BF16)
        gains[u, 0] = jnp.broadcast_to(gin_ref[u : u + 1, :], (128, 128)).T

    def prepare_rest(u):
        wg[u] = wgate_ref[u].astype(F32).T.astype(BF16)
        wo[u] = wout_ref[u].astype(F32).T.astype(BF16)
        gains[u, 1] = jnp.broadcast_to(gout_ref[u : u + 1, :], (128, 128)).T

    prepare_in(0)
    mask_row = jnp.broadcast_to(mask_ref[...].astype(F32)[None, :], (8, 768))
    row_part = pltpu.roll(mask_row, (768 - r * 48) % 768, 1)[:, :128].astype(BF16)
    col_part = pltpu.roll(mask_row, (768 - c * 48) % 768, 1)[:, :128].astype(BF16)
    place = lax.broadcasted_iota(jnp.int32, (128, 128), 0)
    lane = lax.broadcasted_iota(jnp.int32, (128, 128), 1)
    col_masks = [nn(col_part, (place == kh * 16 + (lane & 15)).astype(F32).astype(BF16)) for kh in range(3)]

    def load_rows(q):
        tile_copies[q].wait()
        for ih in range(2):
            ihg = q * 2 + ih
            rows = nn(row_part, (place == ihg * 8 + (lane >> 4)).astype(F32).astype(BF16))
            for kh in range(3):
                maskv[q * 3 + kh, ih] = rows * col_masks[kh]
                block = xbuf[ihg * 8 : ihg * 8 + 8, kh * 16 : kh * 16 + 16, :].reshape(128, 128)
                zt[q * 3 + kh, ih] = block.astype(F32).T

    def load_zt(i):
        return jnp.concatenate([zt[i, 0], zt[i, 1]], axis=1)

    def wide(block):
        return jnp.concatenate([block, block], axis=1)

    def project(u, q, kh, values):
        i = q * 3 + kh
        nrm = norm_rows(values, wide(gains[u, 0]))
        normed[i] = nrm
        mask = jnp.concatenate([maskv[i, 0], maskv[i, 1]], axis=1)[0:1]
        chunk, inner = (q, kh) if u == 0 else (kh, q)
        for side in (1, 0):
            for h in range(2):
                val = nn(wproj[u, 2 * side, h * 64 : h * 64 + 64], nrm)
                gat = nn(wproj[u, 2 * side + 1, h * 64 : h * 64 + 64], nrm)
                y = val * sigmoid(gat) * mask
                if side == 0:
                    y = y.reshape(8, 8, 256)
                    y = jnp.concatenate([y[:, :, :128], y[:, :, 128:]], axis=1).astype(BF16)
                    asend[u, chunk, h * 8 : h * 8 + 8, inner] = y
                else:
                    for ih in range(2):
                        part = y[:, ih * 128 : ih * 128 + 128].astype(BF16).reshape(4, 16, 128)
                        rsend[u, chunk, h * 4 : h * 4 + 4, inner, ih] = part

    def send_left(u, chunk):
        def one(n):
            s = col_peer(n)
            remote(asend.at[u, chunk, s], arecv.at[u, chunk, c], u, COLS_OUT, chunk, r, s).start()

        unrolled(16, one)
        arecv[u, chunk, c] = asend[u, chunk, c]

    def send_right(u, chunk):
        def one(n):
            peer = row_peer(n)
            remote(
                rsend.at[u, chunk, peer], rmid.at[u, chunk, rb], u, RIGHT_ROWS, chunk, peer * 2 + core, c
            ).start()

        unrolled(8, one)
        rmid[u, chunk, rb] = rsend[u, chunk, rb]

    def send_chunk(u, chunk):
        send_right(u, chunk)
        if chunk < AHEAD:
            send_left(u, chunk)

    def gates(u):
        def one(i):
            gate[i] = sigmoid(nn(wg[u], normed[i]))

        loop(9, one)

    def left_out(u, chunk):
        wait_bytes(arecv.at[u, chunk, pl.ds(0, 15)], recv_sem.at[u, COLS_OUT, chunk])

        def one(m):
            ch, inner = m // 3, m % 3
            parts = swap_lanes([arecv[u, chunk, 2 * p + ch, inner].astype(F32) for p in range(8)])
            for il in range(8):
                for ih in range(2):
                    stage[m, pl.ds(ih * 8 + il, 8, stride=16), :] = parts[il][ih * 8 : ih * 8 + 8]

        for m in range(6):
            one(m)

        def pack(d):
            bsend[u, chunk, d] = stage[:, d * 16 : d * 16 + 16, :].astype(BF16)

        for d in range(8):
            pack(d)

        def one_send(n):
            peer = row_peer(n)
            remote(
                bsend.at[u, chunk, peer], brecv.at[u, chunk, rb], u, ROWS_OUT, chunk, peer * 2 + core, c
            ).start()

        unrolled(8, one_send)
        brecv[u, chunk, rb] = bsend[u, chunk, rb]

    def left_copy(chunk):
        part = brecv.at[1, chunk, :, pl.ds((1 - core) * 3, 3)]
        return remote(part, lpair.at[chunk], 1, PAIR, 3 + chunk, rb * 2 + 1 - core, c)

    def left_take(u, chunk):
        wait_bytes(brecv.at[u, chunk, pl.ds(0, 7)], recv_sem.at[u, ROWS_OUT, chunk])
        if u == 1:
            left_copy(chunk).start()

    def left_turn(u, chunk):
        if u == 1:
            left_copy(chunk).wait_recv()
            for k in range(3):
                mine = brecv[u, chunk, :, core * 3 + k].reshape(128, 128)
                theirs = lpair[chunk, :, k].reshape(128, 128)
                lturn[chunk, 0, :, k * 128 : k * 128 + 128] = mine.astype(F32).T.astype(BF16)
                lturn[chunk, 1, :, k * 128 : k * 128 + 128] = theirs.astype(F32).T.astype(BF16)

    def right_mid(u, chunk):
        wait_bytes(rmid.at[u, chunk, pl.ds(0, 7)], recv_sem.at[u, RIGHT_ROWS, chunk])

        def one(inner):
            for g in range(8):
                for ih in range(2):
                    at = (g * 2 + ih) * 16
                    stage_mid[inner, at : at + 16, :] = rmid[u, chunk, g, inner, ih].astype(F32)
            for s in range(16):
                tsend[u, chunk, s, inner] = stage_mid[inner, pl.ds(s, 16, stride=16), :].astype(BF16)

        for inner in range(3):
            one(inner)

        def one_send(n):
            s = col_peer(n)
            remote(tsend.at[u, chunk, s], trecv.at[u, chunk, c], u, RIGHT_COLS, chunk, r, s).start()

        unrolled(16, one_send)
        trecv[u, chunk, c] = tsend[u, chunk, c]

    def right_copy(u, chunk):
        return remote(rmat.at[u, chunk], rpair.at[u, chunk], u, PAIR, chunk, rb * 2 + 1 - core, c)

    def right_in(u, chunk):
        wait_bytes(trecv.at[u, chunk, pl.ds(0, 15)], recv_sem.at[u, RIGHT_COLS, chunk])

        def one(m):
            ch, inner = m // 3, m % 3
            parts = swap_lanes([trecv[u, chunk, 2 * p + ch, inner].astype(F32) for p in range(8)])
            for il in range(8):
                stage[m, pl.ds(il, 16, stride=8), :] = parts[il]
            rmat[u, chunk, m] = stage[m].astype(BF16)

        for m in range(6):
            one(m)
        right_copy(u, chunk).start()

    def product(u, n):
        qi, jh = BLOCKS[n]
        if u == 0:
            left = jnp.concatenate([brecv[u, qi, :, m].reshape(128, 128) for m in range(6)], axis=1)
            mine = jnp.concatenate([rmat[u, jh, m] for m in range(6)], axis=1)
            theirs = jnp.concatenate([rpair[u, jh, m] for m in range(6)], axis=1)
            both = nt(left, jnp.concatenate([mine, theirs], axis=0)).astype(BF16)
            places = (core, 1 - core)
        else:
            mine = jnp.concatenate(
                [rmat[u, jh, 3 * k : 3 * k + 3].reshape(384, 128) for k in range(2)], axis=1
            )
            theirs = jnp.concatenate(
                [rpair[u, jh, 3 * k : 3 * k + 3].reshape(384, 128) for k in range(2)], axis=1
            )
            both = (nn(lturn[qi, 0], mine) + nn(lturn[qi, 1], theirs)).astype(BF16)
            places = (0, 1)
        for k in range(2):
            cbuf[u, :, n, places[k]] = both[:, k * 128 : k * 128 + 128].reshape(8, 16, 128)

    def products(u, w):
        begin, end = WAVES[w]
        for n in range(begin, end):
            product(u, n)
        span = pl.ds(begin, end - begin)

        def one(n):
            peer = row_peer(n)
            remote(
                cbuf.at[u, peer, span], crecv.at[u, rb, span], u, ROWS_BACK, w, peer * 2 + core, c
            ).start()

        unrolled(8, one)
        crecv[u, rb, span] = cbuf[u, rb, span]

    def regroup_back(u, w):
        begin, end = WAVES[w]
        size = end - begin
        span = pl.ds(begin, size)
        wait_bytes(crecv.at[u, pl.ds(0, 7), span], recv_sem.at[u, ROWS_BACK, w])

        def unpack(d):
            stage_back[0:size, :, d * 16 : d * 16 + 16, :] = crecv[u, d, span].astype(F32)

        for d in range(8):
            unpack(d)

        def one(n):
            for ch in range(2):
                rows = [
                    jnp.concatenate(
                        [stage_back[n, ch, pl.ds(ih * 8 + il, 8, stride=16), :] for ih in range(2)], axis=0
                    )
                    for il in range(8)
                ]
                for p, part in enumerate(swap_lanes(rows)):
                    dsend[u, 2 * p + ch, begin + n] = part.astype(BF16)

        for n in range(size):
            one(n)

        def one_send(n):
            s = col_peer(n)
            remote(dsend.at[u, s, span], drecv.at[u, c, span], u, COLS_BACK, w, r, s).start()

        unrolled(16, one_send)
        drecv[u, c, span] = dsend[u, c, span]

    def arrive_back(u, w):
        begin, end = WAVES[w]
        wait_bytes(drecv.at[u, pl.ds(0, 15), pl.ds(begin, end - begin)], recv_sem.at[u, COLS_BACK, w])

    def finish(u, n):
        q, kh = BLOCKS[n]
        i = q * 3 + kh
        got = drecv[u, :, n].astype(F32).reshape(16, 2, 8, 128)
        mixed = jnp.concatenate([got[:, 0].reshape(128, 128), got[:, 1].reshape(128, 128)], axis=1)
        branch = nn(wo[u], norm_rows(mixed, wide(gains[u, 1])))
        new = (load_zt(i) + gate[i] * branch).astype(BF16).astype(F32)
        for ih in range(2):
            half = new[:, ih * 128 : ih * 128 + 128]
            if u == 0:
                zt[i, ih] = half
            else:
                rows = (q * 2 + ih) * 8
                out_ref[rows : rows + 8, kh * 16 : kh * 16 + 16, :] = half.T.astype(BF16).reshape(8, 16, 128)
        if u == 0:
            project(1, q, kh, new)

    def first(q):
        load_rows(q)
        loop(3, lambda kh: project(0, q, kh, load_zt(q * 3 + kh)))

    first(0)
    pl.semaphore_wait(barrier, 23)
    send_chunk(0, 0)
    for q in (1, 2):
        first(q)
        send_chunk(0, q)
    prepare_in(1)
    for u in range(2):
        prepare_rest(u)
    steps = {
        "left": send_left, "gates": lambda u, index: gates(u), "out": left_out, "take": left_take, "turn": left_turn, "mid": right_mid, "in": right_in,
        "pair": lambda u, chunk: right_copy(u, chunk).wait_recv(), "product": products, "back": regroup_back,
        "land": arrive_back, "finish": finish, "next": lambda u, chunk: send_chunk(1, chunk) if u == 0 else None,
    }
    for u in range(2):
        for step, index in PLAN:
            steps[step](u, index)

    for u in range(2):
        for chunk in range(3):
            wait_bytes(asend.at[u, chunk, pl.ds(0, 15)], send_sem.at[u, COLS_OUT, chunk])
            wait_bytes(bsend.at[u, chunk, pl.ds(0, 7)], send_sem.at[u, ROWS_OUT, chunk])
            wait_bytes(rsend.at[u, chunk, pl.ds(0, 7)], send_sem.at[u, RIGHT_ROWS, chunk])
            wait_bytes(tsend.at[u, chunk, pl.ds(0, 15)], send_sem.at[u, RIGHT_COLS, chunk])
            right_copy(u, chunk).wait_send()
            if u == 1:
                left_copy(chunk).wait_send()
        for w, (begin, end) in enumerate(WAVES):
            span = pl.ds(begin, end - begin)
            wait_bytes(cbuf.at[u, pl.ds(0, 7), span], send_sem.at[u, ROWS_BACK, w])
            wait_bytes(dsend.at[u, pl.ds(0, 15), span], send_sem.at[u, COLS_BACK, w])


def body(pair_state, residue_mask, weight_in, weight_gate, weight_out, gain_in, gain_out):
    vmem = pl.BlockSpec(memory_space=pltpu.VMEM)
    weights = weight_in.transpose(0, 2, 1, 3)
    mask = residue_mask
    return pl.pallas_call(
        kernel,
        out_shape=jax.ShapeDtypeStruct((48, 48, 128), BF16),
        in_specs=[pl.BlockSpec(memory_space=pl.ANY)] + [vmem] * 6,
        out_specs=vmem,
        scratch_shapes=[
            pltpu.VMEM((48, 48, 128), BF16),
            pltpu.VMEM((9, 2, 128, 128), F32),
            pltpu.VMEM((9, 128, 256), BF16),
            pltpu.VMEM((9, 128, 256), F32),
            pltpu.VMEM((9, 2, 8, 128), F32),
            pltpu.VMEM((2, 4, 128, 128), BF16),
            pltpu.VMEM((2, 128, 128), BF16),
            pltpu.VMEM((2, 128, 128), BF16),
            pltpu.VMEM((2, 2, 128, 128), F32),
            pltpu.VMEM((2, 3, 16, 3, 16, 128), BF16),
            pltpu.VMEM((2, 3, 16, 3, 16, 128), BF16),
            pltpu.VMEM((2, 3, 8, 6, 16, 128), BF16),
            pltpu.VMEM((2, 3, 8, 6, 16, 128), BF16),
            pltpu.VMEM((2, 3, 8, 3, 2, 16, 128), BF16),
            pltpu.VMEM((2, 3, 8, 3, 2, 16, 128), BF16),
            pltpu.VMEM((2, 3, 16, 3, 16, 128), BF16),
            pltpu.VMEM((2, 3, 16, 3, 16, 128), BF16),
            pltpu.VMEM((2, 3, 6, 128, 128), BF16),
            pltpu.VMEM((2, 3, 6, 128, 128), BF16),
            pltpu.VMEM((3, 8, 3, 16, 128), BF16),
            pltpu.VMEM((3, 2, 128, 384), BF16),
            pltpu.VMEM((2, 8, 9, 2, 16, 128), BF16),
            pltpu.VMEM((2, 8, 9, 2, 16, 128), BF16),
            pltpu.VMEM((2, 16, 9, 16, 128), BF16),
            pltpu.VMEM((2, 16, 9, 16, 128), BF16),
            pltpu.VMEM((6, 128, 128), F32),
            pltpu.VMEM((3, 256, 128), F32),
            pltpu.VMEM((3, 2, 128, 128), F32),
            pltpu.SemaphoreType.DMA((3,)),
            pltpu.SemaphoreType.DMA((2, 7, 6)),
            pltpu.SemaphoreType.DMA((2, 7, 6)),
        ],
        compiler_params=pltpu.CompilerParams(
            collective_id=0, has_side_effects=True, vmem_limit_bytes=48 * 1024 * 1024
        ),
        name="triangle",
    )(pair_state, mask, weights, weight_gate, weight_out, gain_in, gain_out)


def solution(mesh):
    return jax.shard_map(
        body,
        mesh=mesh,
        in_specs=(P("row", "col", None), P(), P(), P(), P(), P(), P()),
        out_specs=P("row", "col", None),
        check_vma=False,
    )
```
